256 devices in a mesh: dp: 4 (over y_hi, core), expert: 64 (over z, x, y_lo).
Axes of the slice: x: 4, y: 4 (y_hi: 2, y_lo: 2; y = y_hi * 2 + y_lo), z: 8, core: 2. Of those that a mesh axis runs over, the one named last changes fastest.
Arguments:
- tokens: bfloat16 [512, 256, 1024], P(('dp', 'expert')), may hold values from -20 to 20
- slot_params: bfloat16 [1024, 128], replicated, may hold values from -1 to 1
- w_in: bfloat16 [128, 1024, 2560], P('expert', None, 'dp'), may hold values from -0.1875 to 0.1875
- w_out: bfloat16 [128, 2560, 1024], P('expert', 'dp'), may hold values from -0.125 to 0.125
- slot_outputs: bfloat16 [512, 128, 1024], P(('dp', 'expert')), may hold values from -6 to 6
- out_grad: bfloat16 [512, 256, 1024], P(('dp', 'expert')), may hold values from -24 to 24
Outputs:
- tokens_grad: bfloat16 [512, 256, 1024], P(('dp', 'expert'))
- params_grad: float32 [1024, 128], replicated
- w_in_grad: bfloat16 [128, 1024, 2560], P('expert', None, 'dp')
- w_out_grad: bfloat16 [128, 2560, 1024], P('expert', 'dp')
The draws below stay inside these ranges and needn't reach their ends.
All inputs are finite; a program needn't handle non-finite values.
Results may differ from the reference program's by a relative error of at most 0.017.
Values may be sent and summed in bfloat16 or wider, within the bound.
No kernel may reach another device: no remote copies, remote signals or barrier semaphores. Data moves between devices by JAX's collectives and lax.ppermute only.
A program may use at most 128 MiB of HBM per device.

```python
import math
import jax
import jax.numpy as jnp
from jax import lax

D = 1024
FF = 2560
PATCH = 256
EXPERTS = 128
FRAMES = 512


def raw_params(key):
    key_gauss = jax.random.fold_in(key, 0)
    key_scale = jax.random.fold_in(key, 2)
    gauss = jax.random.normal(key_gauss, (D, EXPERTS), jnp.float32)
    column_scale = jnp.exp(jax.random.uniform(key_scale, (1, EXPERTS), jnp.float32, math.log(0.3), math.log(3.0)))
    return (gauss, column_scale)


def draw_slot_params(key, part):
    gauss, column_scale = raw_params(key)
    table = gauss * column_scale / math.sqrt(D)
    return jnp.clip(table, -1.0, 1.0).astype(jnp.bfloat16)


def draw_tokens(key, part):
    key = jax.random.fold_in(key, 7)
    key_body, key_row = jax.random.split(key)
    row_scale = jnp.exp(jax.random.uniform(key_row, (FRAMES, PATCH, 1), jnp.float32, math.log(0.4), math.log(4.0)))
    values = jax.random.normal(key_body, (FRAMES, PATCH, D), jnp.float32) * row_scale
    return jnp.clip(values, -20.0, 20.0).astype(jnp.bfloat16)


def block_scale(key, extent, cuts, low, top_value):
    gain = 1.0
    for position, parts in cuts:
        steps = jax.random.uniform(jax.random.fold_in(jax.random.fold_in(key, 6), position), (parts,), jnp.float32, low / len(cuts), top_value / len(cuts))
        gain = gain * jnp.repeat(jnp.exp(steps), extent[position] // parts).reshape((-1,) + (1,) * (len(extent) - 1 - position))
    return gain


def centred(rng, extent, scale, most, cuts=(), dtype=jnp.bfloat16):
    loudness = block_scale(rng, extent, cuts, -0.22, 0.18) if cuts else 1.0
    drawn = jax.random.normal(rng, extent, jnp.float32) * scale * loudness
    return jnp.minimum(jnp.maximum(drawn, -most), most).astype(dtype)


def setup_inputs(seed: int = 0) -> dict:
    keys = jax.random.split(jax.random.key(seed), 7)
    return {
        "tokens": draw_tokens(jax.random.fold_in(keys[6], 71), 0),
        "slot_params": draw_slot_params(jax.random.fold_in(keys[6], 71), 0),
        "w_in": centred(keys[2], (EXPERTS, D, FF), D ** -0.5, 0.1875, ((0, 64), (2, 4))),
        "w_out": centred(keys[3], (EXPERTS, FF, D), FF ** -0.5, 0.125, ((0, 64), (1, 4))),
        "slot_outputs": centred(keys[4], (FRAMES, EXPERTS, D), 1.0, 6.0, ((0, 256),)),
        "out_grad": centred(keys[5], (FRAMES, PATCH, D), 4.0, 24.0, ((0, 256),)),
    }


inv_root_two = 0.7071067811865476
inv_root_tau = 0.3989422804014327


def gelu_parts(hidden_pre):
    cdf = 0.5 * (1.0 + lax.erf(hidden_pre * inv_root_two))
    dens = jnp.exp(-0.5 * hidden_pre * hidden_pre) * inv_root_tau
    return hidden_pre * cdf, cdf + hidden_pre * dens


def one_expert(pieces):
    slot_rows, grad_rows, weight_in, weight_out = pieces
    hidden_pre = jnp.dot(slot_rows, weight_in, preferred_element_type=jnp.float32)
    gelu_out, gelu_slope = gelu_parts(hidden_pre)
    active = gelu_out.astype(jnp.bfloat16)
    act_grad = jnp.dot(grad_rows, weight_out.T, preferred_element_type=jnp.float32)
    pre_grad = (act_grad * gelu_slope).astype(jnp.bfloat16)
    out_weight_grad = jnp.dot(active.T, grad_rows, preferred_element_type=jnp.float32).astype(jnp.bfloat16)
    in_weight_grad = jnp.dot(slot_rows.T, pre_grad, preferred_element_type=jnp.float32).astype(jnp.bfloat16)
    returned_rows = jnp.dot(pre_grad, weight_in.T, preferred_element_type=jnp.float32).astype(jnp.bfloat16)
    return returned_rows, in_weight_grad, out_weight_grad


def reference(tokens, slot_params, w_in, w_out, slot_outputs, out_grad):
    tokens_wide = tokens.astype(jnp.float32)
    params_wide = slot_params.astype(jnp.float32)
    logits = jnp.einsum("fpd,de->fpe", tokens_wide, params_wide)
    dispatch = jax.nn.softmax(logits, axis=1)
    combine = jax.nn.softmax(logits, axis=2)
    dispatch_low = dispatch.astype(jnp.bfloat16)
    combine_low = combine.astype(jnp.bfloat16)
    slots_in = jnp.einsum("fpe,fpd->fed", dispatch_low.astype(jnp.float32), tokens_wide).astype(jnp.bfloat16)
    slot_grad = jnp.einsum("fpe,fpd->fed", combine_low.astype(jnp.float32), out_grad.astype(jnp.float32)).astype(jnp.bfloat16)
    returned_rows, w_in_grad, w_out_grad = lax.map(one_expert, (jnp.swapaxes(slots_in, 0, 1), jnp.swapaxes(slot_grad, 0, 1), w_in, w_out))
    slots_in_grad = jnp.swapaxes(returned_rows, 0, 1)
    combine_grad = jnp.einsum("fpd,fed->fpe", out_grad.astype(jnp.float32), slot_outputs.astype(jnp.float32))
    dispatch_grad = jnp.einsum("fpd,fed->fpe", tokens_wide, slots_in_grad.astype(jnp.float32))
    logits_grad = dispatch * (dispatch_grad - jnp.sum(dispatch * dispatch_grad, axis=1, keepdims=True))
    logits_grad = logits_grad + combine * (combine_grad - jnp.sum(combine * combine_grad, axis=2, keepdims=True))
    logits_low = logits_grad.astype(jnp.bfloat16)
    tokens_grad = jnp.einsum("fpe,fed->fpd", dispatch_low.astype(jnp.float32), slots_in_grad.astype(jnp.float32))
    tokens_grad = tokens_grad + jnp.einsum("fpe,de->fpd", logits_low.astype(jnp.float32), params_wide)
    params_grad = jnp.einsum("fpd,fpe->de", tokens_wide, logits_low.astype(jnp.float32))
    return tokens_grad.astype(jnp.bfloat16), params_grad, w_in_grad, w_out_grad
```

```python
import jax
import jax.numpy as jnp
from jax import lax
from jax.sharding import Mesh, PartitionSpec as P

inv_root_two = 0.7071067811865476
inv_root_tau = 0.3989422804014327

bf16 = jnp.bfloat16
f32 = jnp.float32
Y = ("yh", "yl")
ZX = ("z", "x")
CORE_SWAP = [(0, 1), (1, 0)]


def gelu_parts(hidden_pre):
    cdf = 0.5 * (1.0 + lax.erf(hidden_pre * inv_root_two))
    dens = jnp.exp(-0.5 * hidden_pre * hidden_pre) * inv_root_tau
    return (hidden_pre * cdf, cdf + hidden_pre * dens)


def to_y(value, step):
    return lax.ppermute(value, Y, [(i, (i + step) % 4) for i in range(4)])


def to_core(value):
    return lax.ppermute(value, "core", CORE_SWAP)


def exchange(value):
    return lax.all_to_all(value, ZX, split_axis=0, concat_axis=0, tiled=True)


def to_relative(pair, yl):
    first, second = pair
    return (jnp.where(yl == 0, first, second), jnp.where(yl == 0, second, first))


def spread(slots, yl):
    frames, experts, depth = slots.shape
    groups = experts // 4
    view = slots.reshape(frames, groups, 2, 2, depth)
    own, other = to_relative((view[:, :, 0], view[:, :, 1]), yl)
    message = jnp.stack([own, other], axis=2)
    message = message.transpose(1, 2, 3, 0, 4).reshape(groups, 4 * frames, depth)
    message = exchange(message).reshape(groups, 2, 2, frames, depth)
    message = message.transpose(1, 2, 0, 3, 4).reshape(2, 2, groups * frames, depth)
    own, other = message[0], message[1]
    blocks = [own, to_y(other, 1), to_y(other, -1), to_y(own, 2)]
    far = [to_core(block) for block in blocks]
    return jnp.concatenate(blocks + far, axis=1)


def gather_back(partial, frames, yl):
    _, rows, depth = partial.shape
    size = rows // 8
    groups = size // frames
    near, far = partial[:, : rows // 2], partial[:, rows // 2 :]
    near = near.astype(f32) + to_core(far).astype(f32)
    near = near.astype(bf16)
    own, back, ahead, across = [near[:, i * size : (i + 1) * size] for i in range(4)]
    other = (to_y(back, -1).astype(f32) + to_y(ahead, 1).astype(f32)).astype(bf16)
    own = (own.astype(f32) + to_y(across, 2).astype(f32)).astype(bf16)
    message = jnp.stack([own, other]).reshape(2, 2, groups, frames, depth)
    message = message.transpose(2, 0, 1, 3, 4).reshape(groups, 4 * frames, depth)
    message = exchange(message).reshape(groups, 2, 2, frames, depth)
    first, second = to_relative((message[:, 0], message[:, 1]), yl)
    result = jnp.stack([first, second], axis=1)
    return result.transpose(3, 0, 1, 2, 4).reshape(frames, groups * 4, depth)


def sum_all(value, groups):
    rows, cols = value.shape
    core = lax.axis_index("core")
    y = lax.axis_index("yh") * 2 + lax.axis_index("yl")
    half, part = rows // 2, rows // 8
    low, high = value[:half], value[half:]
    mine = jnp.where(core == 0, low, high)
    theirs = jnp.where(core == 0, high, low).astype(bf16)
    mine = mine + to_core(theirs).astype(f32)

    def block(step):
        return lax.dynamic_slice_in_dim(mine, lax.rem(y + step, 4) * part, part, 0)

    arrived = [to_y(block(step).astype(bf16), step).astype(f32) for step in (1, 3, 2)]
    mine = block(0) + arrived[0] + arrived[1] + arrived[2]
    pieces = exchange(mine.astype(bf16).reshape(groups, part // groups, cols))
    total = jnp.sum(pieces.astype(f32), axis=0).astype(bf16)
    total = exchange(jnp.broadcast_to(total[None], (groups,) + total.shape)).reshape(part, cols)
    ring = [total, to_y(total, 3), to_y(total, 2), to_y(total, 1)]
    ring = jnp.concatenate(ring + ring, axis=0)
    mine = lax.dynamic_slice_in_dim(ring, lax.rem(4 - y, 4) * part, half, 0)
    theirs = to_core(mine)
    low = jnp.where(core == 0, mine, theirs)
    high = jnp.where(core == 0, theirs, mine)
    return jnp.concatenate([low, high], axis=0).astype(f32)


def shards(tokens, slot_params, w_in, w_out, slot_outputs, out_grad):
    frames, groups = tokens.shape[0], slot_params.shape[1] // 4
    yl = lax.axis_index("yl")
    logits = jnp.einsum("fpd,de->fpe", tokens, slot_params, preferred_element_type=f32)
    dispatch = jax.nn.softmax(logits, axis=1)
    combine = jax.nn.softmax(logits, axis=2)
    dispatch_low = dispatch.astype(bf16)
    combine_low = combine.astype(bf16)
    slots_in = jnp.einsum(
        "fpe,fpd->fed", dispatch_low, tokens, preferred_element_type=f32
    ).astype(bf16)
    slot_grad = jnp.einsum(
        "fpe,fpd->fed", combine_low, out_grad, preferred_element_type=f32
    ).astype(bf16)
    slot_rows = spread(slots_in, yl)
    grad_rows = spread(slot_grad, yl)

    hidden_pre = jnp.einsum("erd,edh->erh", slot_rows, w_in, preferred_element_type=f32)
    gelu_out, gelu_slope = gelu_parts(hidden_pre)
    active = gelu_out.astype(bf16)
    act_grad = jnp.einsum("erd,ehd->erh", grad_rows, w_out, preferred_element_type=f32)
    pre_grad = (act_grad * gelu_slope).astype(bf16)
    partial = jnp.einsum("erh,edh->erd", pre_grad, w_in, preferred_element_type=f32)
    slots_in_grad = gather_back(partial.astype(bf16), frames, yl)
    w_out_grad = jnp.einsum(
        "erh,erd->ehd", active, grad_rows, preferred_element_type=f32
    ).astype(bf16)
    w_in_grad = jnp.einsum(
        "erd,erh->edh", slot_rows, pre_grad, preferred_element_type=f32
    ).astype(bf16)

    combine_grad = jnp.einsum(
        "fpd,fed->fpe", out_grad, slot_outputs, preferred_element_type=f32
    )
    combine_part = combine * (
        combine_grad - jnp.sum(combine * combine_grad, axis=2, keepdims=True)
    )
    dispatch_grad = jnp.einsum(
        "fpd,fed->fpe", tokens, slots_in_grad, preferred_element_type=f32
    )
    logits_grad = dispatch * (
        dispatch_grad - jnp.sum(dispatch * dispatch_grad, axis=1, keepdims=True)
    )
    logits_low = (logits_grad + combine_part).astype(bf16)
    params_local = jnp.einsum("fpd,fpe->de", tokens, logits_low, preferred_element_type=f32)
    params_grad = sum_all(params_local, groups)
    tokens_grad = jnp.einsum(
        "fpe,fed->fpd", dispatch_low, slots_in_grad, preferred_element_type=f32
    )
    tokens_grad = tokens_grad + jnp.einsum(
        "fpe,de->fpd", logits_low, slot_params, preferred_element_type=f32
    )
    return (tokens_grad.astype(bf16), params_grad, w_in_grad, w_out_grad)


def split_mesh(mesh):
    experts = mesh.devices.shape[1]
    x = 4 if experts >= 64 else 2
    return Mesh(
        mesh.devices.reshape(2, 2, experts // (2 * x), x, 2), ("yh", "core", "z", "x", "yl")
    )


def solution(mesh):
    dp, expert = ("yh", "core"), ("z", "x", "yl")
    whole = dp + expert
    in_specs = (
        P(whole, None, None),
        P(),
        P(expert, None, dp),
        P(expert, dp, None),
        P(whole, None, None),
        P(whole, None, None),
    )
    out_specs = (
        P(whole, None, None),
        P(),
        P(expert, None, dp),
        P(expert, dp, None),
    )
    return jax.shard_map(
        shards, mesh=split_mesh(mesh), in_specs=in_specs, out_specs=out_specs, check_vma=False
    )
```

```python
import functools

import jax
import jax.numpy as jnp
from jax import lax
from jax.experimental import pallas as pl
from jax.experimental.pallas import tpu as pltpu
from jax.sharding import Mesh, PartitionSpec as P

inv_root_two = 0.7071067811865476
inv_root_tau = 0.3989422804014327

bf16 = jnp.bfloat16
f32 = jnp.float32
Y = ("yh", "yl")
ZX = ("z", "x")
CORE_SWAP = [(0, 1), (1, 0)]
MIB = 1 << 20


def dot(a, b, dims=((1,), (0,))):
    return lax.dot_general(a, b, (dims, ((), ())), preferred_element_type=f32)


def one_hot(test):
    return jnp.where(test, 1.0, 0.0).astype(bf16)


def message_rows(shape, axis, yl, frames):
    row = lax.broadcasted_iota(jnp.int32, shape, axis)
    frame = row & (frames - 1)
    rest = row // frames
    expert = (rest // 4) * 4 + ((((rest // 2) & 1) ^ yl) * 2) + (rest & 1)
    return frame * (shape[axis] // frames) + expert


def call(kernel, out_shape, *args, grid=(), in_specs=None, out_specs=None, vmem=16, flops=0, **kw):
    nbytes = sum(a.size * a.dtype.itemsize for a in args)
    nbytes += sum(o.size * o.dtype.itemsize for o in jax.tree.leaves(out_shape))
    if in_specs is None:
        in_specs = [pl.BlockSpec(memory_space=pltpu.VMEM) for _ in args]
    if out_specs is None:
        out_specs = jax.tree.map(lambda _: pl.BlockSpec(memory_space=pltpu.VMEM), out_shape)
    return pl.pallas_call(
        kernel,
        out_shape=out_shape,
        grid=grid,
        in_specs=in_specs,
        out_specs=out_specs,
        compiler_params=pltpu.CompilerParams(vmem_limit_bytes=vmem * MIB),
        cost_estimate=pl.CostEstimate(flops=flops, bytes_accessed=nbytes, transcendentals=0),
        **kw,
    )(*args)


def shape(dims, dtype):
    return jax.ShapeDtypeStruct(dims, dtype)


SMEM = pl.BlockSpec(memory_space=pltpu.SMEM)
VMEM = pl.BlockSpec(memory_space=pltpu.VMEM)
ANY = pl.BlockSpec(memory_space=pl.ANY)


def to_message(place_ref, slots, out_ref):
    rows = out_ref.shape[0]
    yl = place_ref[0]
    order = one_hot(
        message_rows((rows, rows), 0, yl, len(slots)) == lax.broadcasted_iota(jnp.int32, (rows, rows), 1)
    )
    out_ref[...] = dot(order, jnp.concatenate(slots, axis=0)).astype(bf16)


def prep_kernel(place_ref, tokens_ref, params_ref, message_ref, dispatch_ref, combine_ref):
    slots = []
    for f in range(tokens_ref.shape[0]):
        tokens = tokens_ref[f]
        logits = dot(tokens, params_ref[...])
        up = jnp.exp(logits - jnp.max(logits, axis=0, keepdims=True))
        dispatch = up / jnp.sum(up, axis=0, keepdims=True)
        dispatch_ref[f] = dispatch
        slots.append(dot(dispatch.astype(bf16), tokens, ((0,), (0,))).astype(bf16))
        up = jnp.exp(logits - jnp.max(logits, axis=1, keepdims=True))
        combine_ref[f] = up / jnp.sum(up, axis=1, keepdims=True)
    to_message(place_ref, slots, message_ref)


def grad_kernel(place_ref, combine_ref, out_grad_ref, message_ref):
    slots = []
    for f in range(out_grad_ref.shape[0]):
        low = combine_ref[f].astype(bf16)
        slots.append(dot(low, out_grad_ref[f], ((0,), (0,))).astype(bf16))
    to_message(place_ref, slots, message_ref)


def sort_order(rows, frames, axis):
    row = lax.broadcasted_iota(jnp.int32, (rows, rows), axis)
    pair = row // (rows // 4)
    rest = row - pair * (rows // 4)
    return (rest // frames) * (4 * frames) + pair * frames + (rest & (frames - 1))


def sort_kernel(frames, message_ref, own_ref, other_ref):
    rows, depth = message_ref.shape
    order = one_hot(
        sort_order(rows, frames, 0) == lax.broadcasted_iota(jnp.int32, (rows, rows), 1)
    )
    out = dot(order, message_ref[...]).astype(bf16)
    own_ref[...] = out[: rows // 2].reshape(own_ref.shape)
    other_ref[...] = out[rows // 2 :].reshape(other_ref.shape)


def unsort_kernel(frames, own_ref, across_ref, back_ref, ahead_ref, message_ref):
    rows, depth = message_ref.shape

    def total(a, b):
        value = a[...].astype(f32) + b[...].astype(f32)
        return value.reshape(rows // 2, depth).astype(bf16)

    value = jnp.concatenate([total(own_ref, across_ref), total(back_ref, ahead_ref)], axis=0)
    order = one_hot(
        sort_order(rows, frames, 1) == lax.broadcasted_iota(jnp.int32, (rows, rows), 0)
    )
    message_ref[...] = dot(order, value).astype(bf16)


def hidden_kernel(*refs):
    pieces, w_in_ref, rows_ref, hidden_ref = refs[:8], refs[8], refs[9], refs[10]
    rows = jnp.concatenate([piece[0] for piece in pieces], axis=0)
    rows_ref[0] = rows
    hidden_ref[0] = dot(rows, w_in_ref[0])


def expert_kernel(*refs):
    pieces, hidden_ref, w_in_ref, w_out_ref = refs[:4], refs[4], refs[5], refs[6]
    rows_ref, active_ref, pre_ref, partial_ref = refs[-4:]
    rows = jnp.concatenate([piece[0] for piece in pieces], axis=0)
    rows_ref[0] = rows
    hidden = hidden_ref[0]
    cdf = 0.5 * (1.0 + lax.erf(hidden * inv_root_two))
    dens = jnp.exp(-0.5 * hidden * hidden) * inv_root_tau
    active_ref[0] = (hidden * cdf).astype(bf16)
    act_grad = dot(rows, w_out_ref[0], ((1,), (1,)))
    pre = (act_grad * (cdf + hidden * dens)).astype(bf16)
    pre_ref[0] = pre
    partial = dot(pre, w_in_ref[0], ((1,), (1,)))
    partial_ref[...] = partial.astype(partial_ref.dtype).reshape(partial_ref.shape)


def tail_kernel(place_ref, message_ref, tokens_ref, dispatch_ref, part_ref, slots_ref, low_ref, mine_ref, theirs_ref, sum_ref):
    rows, depth = message_ref.shape
    frames, experts = slots_ref.shape[:2]
    order = one_hot(
        message_rows((rows, rows), 1, place_ref[0], frames)
        == lax.broadcasted_iota(jnp.int32, (rows, rows), 0)
    )
    slots = dot(order, message_ref[...]).astype(bf16)
    total = None
    for f in range(frames):
        mine = slots[f * experts : (f + 1) * experts]
        slots_ref[f] = mine
        tokens = tokens_ref[f]
        dispatch = dispatch_ref[f]
        slope = dot(tokens, mine, ((1,), (1,)))
        slope = slope - jnp.sum(dispatch * slope, axis=0, keepdims=True)
        low = (dispatch * slope + part_ref[f]).astype(bf16)
        low_ref[f] = low
        term = dot(low, tokens, ((0,), (0,)))
        total = term if total is None else total + term
    sum_ref[...] = total.T
    half = depth // 2
    core = place_ref[1]
    mine_ref[...] = sum_ref[pl.ds(pl.multiple_of(core * half, half), half), :]
    theirs_ref[...] = sum_ref[pl.ds(pl.multiple_of((1 - core) * half, half), half), :].astype(bf16)


def tokens_kernel(dispatch_ref, low_ref, slots_ref, params_ref, out_ref):
    params = params_ref[...].T
    for f in range(out_ref.shape[0]):
        left = jnp.concatenate([dispatch_ref[f].astype(bf16), low_ref[f]], axis=1)
        right = jnp.concatenate([slots_ref[f], params], axis=0)
        out_ref[f] = dot(left, right).astype(bf16)


def to_y(value, step):
    return lax.ppermute(value, Y, [(i, (i + step) % 4) for i in range(4)])


def to_core(value):
    return lax.ppermute(value, "core", CORE_SWAP)


def exchange(value):
    return lax.all_to_all(value, ZX, split_axis=0, concat_axis=0, tiled=True)


def spread(message, groups, frames):
    rows, depth = message.shape
    message = exchange(message.reshape(groups, rows // groups, depth)).reshape(rows, depth)
    half = shape((2, rows // 4, depth), bf16)
    own, other = call(
        functools.partial(sort_kernel, frames), (half, half), message, flops=2 * rows * rows * depth
    )
    near = [own, to_y(other, 1), to_y(other, -1), to_y(own, 2)]
    return near, [to_core(piece) for piece in near]


def sum_all(mine, theirs, groups, beside):
    half, cols = mine.shape
    core = lax.axis_index("core")
    mine = (mine + to_core(theirs).astype(f32)).astype(bf16)
    pieces = exchange(mine.reshape(groups, half // groups, cols))
    part = jnp.sum(pieces.astype(f32), axis=0)
    across, back, ahead = to_y(part, 2), to_y(part, 1), to_y(part, -1)
    across, beside = lax.optimization_barrier((across, beside))
    total = ((part + across) + (back + ahead)).astype(bf16)
    mine = exchange(jnp.broadcast_to(total[None], (groups,) + total.shape)).reshape(half, cols)
    theirs = to_core(mine)
    low = jnp.where(core == 0, mine, theirs)
    high = jnp.where(core == 0, theirs, mine)
    return jnp.concatenate([low, high], axis=0).astype(f32), beside


def shards(tokens, slot_params, w_in, w_out, slot_outputs, out_grad):
    frames, patch, depth = tokens.shape
    experts = slot_params.shape[1]
    hidden_size = w_in.shape[2]
    groups = experts // 4
    rows = frames * experts
    block = rows // 4
    place = jnp.stack([lax.axis_index("yl"), lax.axis_index("core")]).astype(jnp.int32)
    frame_flops = 2 * frames * patch * experts * depth
    sort_flops = 2 * rows * rows * depth

    message, dispatch, combine = call(
        prep_kernel,
        (
            shape((rows, depth), bf16),
            shape((frames, patch, experts), f32),
            shape((frames, patch, experts), f32),
        ),
        place, tokens, slot_params,
        in_specs=[SMEM, VMEM, VMEM], flops=2 * frame_flops + sort_flops,
    )
    near_in, far_in = spread(message, groups, frames)
    message = call(
        grad_kernel, shape((rows, depth), bf16), place, combine, out_grad,
        in_specs=[SMEM, VMEM, VMEM], flops=frame_flops + sort_flops,
    )
    near_grad, far_grad = spread(message, groups, frames)

    combine_grad = jnp.einsum(
        "fpd,fed->fpe", out_grad, slot_outputs, preferred_element_type=f32
    )
    combine_part = combine * (
        combine_grad - jnp.sum(combine * combine_grad, axis=2, keepdims=True)
    )

    piece = pl.BlockSpec((1, block, depth), lambda e: (e, 0, 0))
    w_in_spec = pl.BlockSpec((1, depth, hidden_size), lambda e: (e, 0, 0))
    w_out_spec = pl.BlockSpec((1, hidden_size, depth), lambda e: (e, 0, 0))
    matmul_flops = 2 * 2 * 8 * block * depth * hidden_size
    slot_rows, hidden = call(
        hidden_kernel,
        (shape((2, 8 * block, depth), bf16), shape((2, 8 * block, hidden_size), f32)),
        *near_in, *far_in, w_in,
        grid=(2,),
        in_specs=[piece] * 8 + [w_in_spec],
        out_specs=(
            pl.BlockSpec((1, 8 * block, depth), lambda e: (e, 0, 0)),
            pl.BlockSpec((1, 8 * block, hidden_size), lambda e: (e, 0, 0)),
        ),
        vmem=20, flops=matmul_flops,
    )

    hidden, combine_part = lax.optimization_barrier((hidden, combine_part))

    def expert_half(half, pieces, filled):
        rows_spec = pl.BlockSpec((1, 4 * block, depth), lambda e: (e, half, 0))
        hidden_spec = pl.BlockSpec((1, 4 * block, hidden_size), lambda e: (e, half, 0))
        return call(
            expert_kernel,
            (
                shape((2, 8 * block, depth), bf16),
                shape((2, 8 * block, hidden_size), bf16),
                shape((2, 8 * block, hidden_size), bf16),
                shape((4, 2, block, depth), bf16 if half else f32),
            ),
            *pieces, hidden, w_in, w_out, *filled,
            grid=(2,),
            in_specs=[piece] * 4 + [hidden_spec, w_in_spec, w_out_spec] + [ANY] * len(filled),
            out_specs=(
                rows_spec,
                hidden_spec,
                hidden_spec,
                pl.BlockSpec((4, 1, block, depth), lambda e: (0, e, 0, 0)),
            ),
            vmem=24, flops=matmul_flops,
            input_output_aliases={7 + i: i for i in range(len(filled))},
        )

    *filled, far = expert_half(1, far_grad, ())
    far = to_core(far)
    grad_rows, active, pre_grad, near = expert_half(0, near_grad, filled)

    def summed(i):
        return (near[i] + far[i].astype(f32)).astype(bf16)

    back, ahead, across, own = summed(1), summed(2), summed(3), summed(0)
    back, ahead, across = to_y(back, -1), to_y(ahead, 1), to_y(across, 2)
    w_out_grad = jnp.einsum(
        "erh,erd->ehd", active, grad_rows, preferred_element_type=f32
    ).astype(bf16)
    w_in_grad = jnp.einsum(
        "erd,erh->edh", slot_rows, pre_grad, preferred_element_type=f32
    ).astype(bf16)
    own, w_in_grad = lax.optimization_barrier((own, w_in_grad))
    message = call(
        functools.partial(unsort_kernel, frames), shape((rows, depth), bf16),
        own, across, back, ahead, flops=sort_flops,
    )
    message = exchange(message.reshape(groups, rows // groups, depth)).reshape(rows, depth)
    message, w_out_grad = lax.optimization_barrier((message, w_out_grad))

    slots_in_grad, logits_low, mine, theirs = call(
        tail_kernel,
        (
            shape((frames, experts, depth), bf16),
            shape((frames, patch, experts), bf16),
            shape((depth // 2, experts), f32),
            shape((depth // 2, experts), bf16),
        ),
        place, message, tokens, dispatch, combine_part,
        in_specs=[SMEM, VMEM, VMEM, VMEM, VMEM],
        scratch_shapes=[pltpu.VMEM((depth, experts), f32)],
        flops=2 * frame_flops + sort_flops,
    )
    tokens_grad = call(
        tokens_kernel, shape((frames, patch, depth), bf16),
        dispatch, logits_low, slots_in_grad, slot_params, flops=2 * frame_flops,
    )
    params_grad, tokens_grad = sum_all(mine, theirs, groups, tokens_grad)
    return (tokens_grad, params_grad, w_in_grad, w_out_grad)


def split_mesh(mesh):
    experts = mesh.devices.shape[1]
    x = 4 if experts >= 64 else 2
    return Mesh(
        mesh.devices.reshape(2, 2, experts // (2 * x), x, 2), ("yh", "core", "z", "x", "yl")
    )


def solution(mesh):
    dp, expert = ("yh", "core"), ("z", "x", "yl")
    whole = dp + expert
    in_specs = (
        P(whole, None, None),
        P(),
        P(expert, None, dp),
        P(expert, dp, None),
        P(whole, None, None),
        P(whole, None, None),
    )
    out_specs = (
        P(whole, None, None),
        P(),
        P(expert, None, dp),
        P(expert, dp, None),
    )
    return jax.shard_map(
        shards, mesh=split_mesh(mesh), in_specs=in_specs, out_specs=out_specs, check_vma=False
    )
```

```python
import functools

import jax
import jax.numpy as jnp
from jax import lax
from jax.experimental import pallas as pl
from jax.experimental.pallas import tpu as pltpu
from jax.sharding import Mesh, PartitionSpec as P

inv_root_two = 0.7071067811865476
inv_root_tau = 0.3989422804014327

bf16 = jnp.bfloat16
f32 = jnp.float32
Y = ("yh", "yl")
ZX = ("z", "x")
CORE_SWAP = [(0, 1), (1, 0)]
MIB = 1 << 20


def dot(a, b, dims=((1,), (0,))):
    return lax.dot_general(a, b, (dims, ((), ())), preferred_element_type=f32)


def one_hot(test):
    return jnp.where(test, 1.0, 0.0).astype(bf16)


def message_rows(shape, axis, yl, frames, arrays):
    row = lax.broadcasted_iota(jnp.int32, shape, axis)
    experts = shape[axis] // (frames * arrays)
    frame = row & (frames - 1)
    rest = row // frames
    pair = rest & 1
    array = (rest // 2) & (arrays - 1)
    rest = rest // (2 * arrays)
    expert = (rest // 2) * 4 + ((rest & 1) ^ yl) * 2 + pair
    return (array * frames + frame) * experts + expert


def call(kernel, out_shape, *args, grid=(), in_specs=None, out_specs=None, vmem=16, flops=0, **kw):
    nbytes = sum(a.size * a.dtype.itemsize for a in args)
    nbytes += sum(o.size * o.dtype.itemsize for o in jax.tree.leaves(out_shape))
    if in_specs is None:
        in_specs = [pl.BlockSpec(memory_space=pltpu.VMEM) for _ in args]
    if out_specs is None:
        out_specs = jax.tree.map(lambda _: pl.BlockSpec(memory_space=pltpu.VMEM), out_shape)
    return pl.pallas_call(
        kernel,
        out_shape=out_shape,
        grid=grid,
        in_specs=in_specs,
        out_specs=out_specs,
        compiler_params=pltpu.CompilerParams(vmem_limit_bytes=vmem * MIB),
        cost_estimate=pl.CostEstimate(flops=flops, bytes_accessed=nbytes, transcendentals=0),
        **kw,
    )(*args)


def shape(dims, dtype):
    return jax.ShapeDtypeStruct(dims, dtype)


SMEM = pl.BlockSpec(memory_space=pltpu.SMEM)
VMEM = pl.BlockSpec(memory_space=pltpu.VMEM)
ANY = pl.BlockSpec(memory_space=pl.ANY)


def load(source, target, sems, i):
    copy = pltpu.make_async_copy(source, target, sems.at[i])
    copy.start()
    return copy


def softmax(logits, axis):
    up = jnp.exp(logits - jnp.max(logits, axis=axis, keepdims=True))
    return up / jnp.sum(up, axis=axis, keepdims=True)


def prep_kernel(
    place_ref, params_hbm, tokens_hbm, out_grad_hbm, message_ref, dispatch_ref, combine_ref,
    params_ref, tokens_ref, out_grad_ref, sems,
):
    frames = tokens_ref.shape[0]
    rows = message_ref.shape[0]
    copies = [load(params_hbm, params_ref, sems, 2 * frames)]
    copies += [load(tokens_hbm.at[f], tokens_ref.at[f], sems, f) for f in range(frames)]
    copies += [load(out_grad_hbm.at[f], out_grad_ref.at[f], sems, frames + f) for f in range(frames)]
    order = one_hot(
        message_rows((rows, rows), 0, place_ref[0], frames, 2)
        == lax.broadcasted_iota(jnp.int32, (rows, rows), 1)
    )
    copies[0].wait()
    slots_in, slot_grad = [], []
    for f in range(frames):
        copies[1 + f].wait()
        tokens = tokens_ref[f]
        logits = dot(tokens, params_ref[...])
        dispatch = softmax(logits, 0)
        combine = softmax(logits, 1)
        dispatch_ref[f] = dispatch
        combine_ref[f] = combine
        slots_in.append(dot(dispatch.astype(bf16), tokens, ((0,), (0,))).astype(bf16))
        copies[1 + frames + f].wait()
        slot_grad.append(dot(combine.astype(bf16), out_grad_ref[f], ((0,), (0,))).astype(bf16))
    message_ref[...] = dot(order, jnp.concatenate(slots_in + slot_grad, axis=0)).astype(bf16)


def sort_order(rows, frames, arrays, axis):
    row = lax.broadcasted_iota(jnp.int32, (rows, rows), axis)
    kinds = 4 * arrays
    kind = row // (rows // kinds)
    rest = row - kind * (rows // kinds)
    return (rest // frames) * (kinds * frames) + kind * frames + (rest & (frames - 1))


def sort_kernel(frames, message_ref, *out_refs):
    rows, depth = message_ref.shape
    order = one_hot(
        sort_order(rows, frames, 2, 0) == lax.broadcasted_iota(jnp.int32, (rows, rows), 1)
    )
    out = dot(order, message_ref[...]).astype(bf16)
    part = rows // len(out_refs)
    for i, out_ref in enumerate(out_refs):
        out_ref[...] = out[i * part : (i + 1) * part].reshape(out_ref.shape)


def unsort_kernel(frames, own_ref, across_ref, back_ref, ahead_ref, message_ref):
    rows, depth = message_ref.shape

    def total(a, b):
        value = a[...].astype(f32) + b[...].astype(f32)
        return value.reshape(rows // 2, depth).astype(bf16)

    value = jnp.concatenate([total(own_ref, across_ref), total(back_ref, ahead_ref)], axis=0)
    order = one_hot(
        sort_order(rows, frames, 1, 1) == lax.broadcasted_iota(jnp.int32, (rows, rows), 0)
    )
    message_ref[...] = dot(order, value).astype(bf16)


def hidden_kernel(*refs):
    pieces, w_in_ref, rows_ref, active_ref, slope_ref = refs[:8], *refs[8:]
    rows = jnp.concatenate([piece[0] for piece in pieces], axis=0)
    rows_ref[0] = rows
    hidden = dot(rows, w_in_ref[0])
    cdf = 0.5 * (1.0 + lax.erf(hidden * inv_root_two))
    dens = jnp.exp(-0.5 * hidden * hidden) * inv_root_tau
    active_ref[0] = (hidden * cdf).astype(bf16)
    slope_ref[0] = (cdf + hidden * dens).astype(slope_ref.dtype)


def expert_kernel(*refs):
    pieces, slope_ref, w_in_ref, w_out_ref = refs[:4], refs[4], refs[5], refs[6]
    rows_ref, pre_ref, partial_ref = refs[-3:]
    rows = jnp.concatenate([piece[0] for piece in pieces], axis=0)
    rows_ref[0] = rows
    act_grad = dot(rows, w_out_ref[0], ((1,), (1,)))
    pre = (act_grad * slope_ref[0].astype(f32)).astype(bf16)
    pre_ref[0] = pre
    partial = dot(pre, w_in_ref[0], ((1,), (1,)))
    partial_ref[...] = partial.astype(partial_ref.dtype).reshape(partial_ref.shape)


def tail_kernel(place_ref, message_ref, tokens_ref, dispatch_ref, part_ref, slots_ref, low_ref, mine_ref, theirs_ref, sum_ref):
    rows, depth = message_ref.shape
    frames, experts = slots_ref.shape[:2]
    order = one_hot(
        message_rows((rows, rows), 1, place_ref[0], frames, 1)
        == lax.broadcasted_iota(jnp.int32, (rows, rows), 0)
    )
    slots = dot(order, message_ref[...]).astype(bf16)
    total = None
    for f in range(frames):
        mine = slots[f * experts : (f + 1) * experts]
        slots_ref[f] = mine
        tokens = tokens_ref[f]
        dispatch = dispatch_ref[f]
        slope = dot(tokens, mine, ((1,), (1,)))
        slope = slope - jnp.sum(dispatch * slope, axis=0, keepdims=True)
        low = (dispatch * slope + part_ref[f]).astype(bf16)
        low_ref[f] = low
        term = dot(low, tokens, ((0,), (0,)))
        total = term if total is None else total + term
    sum_ref[...] = total.T
    half = depth // 2
    core = place_ref[1]
    mine_ref[...] = sum_ref[pl.ds(pl.multiple_of(core * half, half), half), :]
    theirs_ref[...] = sum_ref[pl.ds(pl.multiple_of((1 - core) * half, half), half), :].astype(bf16)


def tokens_kernel(dispatch_ref, low_ref, slots_ref, params_ref, out_ref):
    params = params_ref[...].T
    for f in range(out_ref.shape[0]):
        left = jnp.concatenate([dispatch_ref[f].astype(bf16), low_ref[f]], axis=1)
        right = jnp.concatenate([slots_ref[f], params], axis=0)
        out_ref[f] = dot(left, right).astype(bf16)


def to_y(value, step):
    return lax.ppermute(value, Y, [(i, (i + step) % 4) for i in range(4)])


def to_core(value):
    return lax.ppermute(value, "core", CORE_SWAP)


def exchange(value):
    return lax.all_to_all(value, ZX, split_axis=0, concat_axis=0, tiled=True)


def sum_all(mine, theirs, groups, beside):
    half, cols = mine.shape
    core = lax.axis_index("core")
    mine = (mine + to_core(theirs).astype(f32)).astype(bf16)
    pieces = exchange(mine.reshape(groups, half // groups, cols))
    pieces, beside = lax.optimization_barrier((pieces, beside))
    part = jnp.sum(pieces.astype(f32), axis=0)
    across, back, ahead = to_y(part, 2), to_y(part, 1), to_y(part, -1)
    total = ((part + across) + (back + ahead)).astype(bf16)
    mine = exchange(jnp.broadcast_to(total[None], (groups,) + total.shape)).reshape(half, cols)
    theirs = to_core(mine)
    low = jnp.where(core == 0, mine, theirs)
    high = jnp.where(core == 0, theirs, mine)
    return jnp.concatenate([low, high], axis=0).astype(f32), beside


def shards(tokens, slot_params, w_in, w_out, slot_outputs, out_grad):
    frames, patch, depth = tokens.shape
    experts = slot_params.shape[1]
    hidden_size = w_in.shape[2]
    groups = experts // 4
    rows = frames * experts
    block = rows // 4
    place = jnp.stack([lax.axis_index("yl"), lax.axis_index("core")]).astype(jnp.int32)
    frame_flops = 2 * frames * patch * experts * depth
    sort_flops = 2 * rows * rows * depth

    message, dispatch, combine = call(
        prep_kernel,
        (
            shape((2 * rows, depth), bf16),
            shape((frames, patch, experts), f32),
            shape((frames, patch, experts), f32),
        ),
        place, slot_params, tokens, out_grad,
        in_specs=[SMEM, ANY, ANY, ANY], vmem=56, flops=3 * frame_flops + 4 * sort_flops,
        scratch_shapes=[
            pltpu.VMEM((depth, experts), bf16),
            pltpu.VMEM((frames, patch, depth), bf16),
            pltpu.VMEM((frames, patch, depth), bf16),
            pltpu.SemaphoreType.DMA((2 * frames + 1,)),
        ],
    )
    message = exchange(message.reshape(groups, 2 * rows // groups, depth)).reshape(2 * rows, depth)

    combine_grad = jnp.einsum(
        "fpd,fed->fpe", out_grad, slot_outputs, preferred_element_type=f32
    )
    combine_part = combine * (
        combine_grad - jnp.sum(combine * combine_grad, axis=2, keepdims=True)
    )
    message, combine_part = lax.optimization_barrier((message, combine_part))

    own_in, own_grad, other_in, other_grad = call(
        functools.partial(sort_kernel, frames), (shape((2, block, depth), bf16),) * 4, message,
        flops=4 * sort_flops,
    )
    near_in = [own_in, to_y(other_in, 1), to_y(other_in, -1), to_y(own_in, 2)]
    near_grad = [own_grad, to_y(other_grad, 1), to_y(other_grad, -1), to_y(own_grad, 2)]
    far_in = [to_core(piece) for piece in near_in]
    far_own = to_core(own_grad)

    piece = pl.BlockSpec((1, block, depth), lambda e: (e, 0, 0))
    w_in_spec = pl.BlockSpec((1, depth, hidden_size), lambda e: (e, 0, 0))
    w_out_spec = pl.BlockSpec((1, hidden_size, depth), lambda e: (e, 0, 0))
    matmul_flops = 2 * 2 * 8 * block * depth * hidden_size
    slot_rows, active, slope = call(
        hidden_kernel,
        (
            shape((2, 8 * block, depth), bf16),
            shape((2, 8 * block, hidden_size), bf16),
            shape((2, 8 * block, hidden_size), bf16),
        ),
        *near_in, *far_in, w_in,
        grid=(2,),
        in_specs=[piece] * 8 + [w_in_spec],
        out_specs=(
            pl.BlockSpec((1, 8 * block, depth), lambda e: (e, 0, 0)),
            pl.BlockSpec((1, 8 * block, hidden_size), lambda e: (e, 0, 0)),
            pl.BlockSpec((1, 8 * block, hidden_size), lambda e: (e, 0, 0)),
        ),
        vmem=24, flops=matmul_flops,
    )
    slope, *arrived = lax.optimization_barrier((slope, *near_grad[1:]))
    near_grad = [own_grad, *arrived]
    far_grad = [far_own] + [to_core(piece) for piece in arrived]

    def expert_half(half, pieces, filled):
        rows_spec = pl.BlockSpec((1, 4 * block, depth), lambda e: (e, half, 0))
        hidden_spec = pl.BlockSpec((1, 4 * block, hidden_size), lambda e: (e, half, 0))
        return call(
            expert_kernel,
            (
                shape((2, 8 * block, depth), bf16),
                shape((2, 8 * block, hidden_size), bf16),
                shape((4, 2, block, depth), bf16 if half else f32),
            ),
            *pieces, slope, w_in, w_out, *filled,
            grid=(2,),
            in_specs=[piece] * 4 + [hidden_spec, w_in_spec, w_out_spec] + [ANY] * len(filled),
            out_specs=(
                rows_spec,
                hidden_spec,
                pl.BlockSpec((4, 1, block, depth), lambda e: (0, e, 0, 0)),
            ),
            vmem=24, flops=matmul_flops,
            input_output_aliases={7 + i: i for i in range(len(filled))},
        )

    *filled, far = expert_half(1, far_grad, ())
    far = to_core(far)
    grad_rows, pre_grad, near = expert_half(0, near_grad, filled)

    def summed(i):
        return (near[i] + far[i].astype(f32)).astype(bf16)

    back, ahead, across, own = summed(1), summed(2), summed(3), summed(0)
    back, ahead, across = to_y(back, -1), to_y(ahead, 1), to_y(across, 2)
    w_out_grad = jnp.einsum(
        "erh,erd->ehd", active, grad_rows, preferred_element_type=f32
    ).astype(bf16)
    w_in_grad = jnp.einsum(
        "erd,erh->edh", slot_rows, pre_grad, preferred_element_type=f32
    ).astype(bf16)
    own, w_in_grad = lax.optimization_barrier((own, w_in_grad))
    message = call(
        functools.partial(unsort_kernel, frames), shape((rows, depth), bf16),
        own, across, back, ahead, flops=sort_flops,
    )
    message = exchange(message.reshape(groups, rows // groups, depth)).reshape(rows, depth)
    message, w_out_grad = lax.optimization_barrier((message, w_out_grad))

    slots_in_grad, logits_low, mine, theirs = call(
        tail_kernel,
        (
            shape((frames, experts, depth), bf16),
            shape((frames, patch, experts), bf16),
            shape((depth // 2, experts), f32),
            shape((depth // 2, experts), bf16),
        ),
        place, message, tokens, dispatch, combine_part,
        in_specs=[SMEM, VMEM, VMEM, VMEM, VMEM],
        scratch_shapes=[pltpu.VMEM((depth, experts), f32)],
        flops=2 * frame_flops + sort_flops,
    )
    tokens_grad = call(
        tokens_kernel, shape((frames, patch, depth), bf16),
        dispatch, logits_low, slots_in_grad, slot_params, flops=2 * frame_flops,
    )
    params_grad, tokens_grad = sum_all(mine, theirs, groups, tokens_grad)
    return (tokens_grad, params_grad, w_in_grad, w_out_grad)


def split_mesh(mesh):
    experts = mesh.devices.shape[1]
    x = 4 if experts >= 64 else 2
    return Mesh(
        mesh.devices.reshape(2, 2, experts // (2 * x), x, 2), ("yh", "core", "z", "x", "yl")
    )


def solution(mesh):
    dp, expert = ("yh", "core"), ("z", "x", "yl")
    whole = dp + expert
    in_specs = (
        P(whole, None, None),
        P(),
        P(expert, None, dp),
        P(expert, dp, None),
        P(whole, None, None),
        P(whole, None, None),
    )
    out_specs = (
        P(whole, None, None),
        P(),
        P(expert, None, dp),
        P(expert, dp, None),
    )
    return jax.shard_map(
        shards, mesh=split_mesh(mesh), in_specs=in_specs, out_specs=out_specs, check_vma=False
    )
```

```python
import functools

import jax
import jax.numpy as jnp
from jax import lax
from jax.experimental import pallas as pl
from jax.experimental.pallas import tpu as pltpu
from jax.sharding import Mesh, PartitionSpec as P

inv_root_two = 0.7071067811865476
inv_root_tau = 0.3989422804014327

bf16 = jnp.bfloat16
f32 = jnp.float32
Y = ("yh", "yl")
ZX = ("z", "x")
PLANE = ("yh", "core", "x", "yl")
CORE_SWAP = [(0, 1), (1, 0)]
MIB = 1 << 20


def dot(a, b, dims=((1,), (0,))):
    return lax.dot_general(a, b, (dims, ((), ())), preferred_element_type=f32)


def one_hot(test):
    return jnp.where(test, 1.0, 0.0).astype(bf16)


def message_rows(shape, axis, yl, frames, arrays):
    row = lax.broadcasted_iota(jnp.int32, shape, axis)
    experts = shape[axis] // (frames * arrays)
    frame = row & (frames - 1)
    rest = row // frames
    pair = rest & 1
    array = (rest // 2) & (arrays - 1)
    rest = rest // (2 * arrays)
    expert = (rest // 2) * 4 + ((rest & 1) ^ yl) * 2 + pair
    return (array * frames + frame) * experts + expert


def call(kernel, out_shape, *args, grid=(), in_specs=None, out_specs=None, vmem=16, flops=0, **kw):
    nbytes = sum(a.size * a.dtype.itemsize for a in args)
    nbytes += sum(o.size * o.dtype.itemsize for o in jax.tree.leaves(out_shape))
    if in_specs is None:
        in_specs = [pl.BlockSpec(memory_space=pltpu.VMEM) for _ in args]
    if out_specs is None:
        out_specs = jax.tree.map(lambda _: pl.BlockSpec(memory_space=pltpu.VMEM), out_shape)
    return pl.pallas_call(
        kernel,
        out_shape=out_shape,
        grid=grid,
        in_specs=in_specs,
        out_specs=out_specs,
        compiler_params=pltpu.CompilerParams(vmem_limit_bytes=vmem * MIB),
        cost_estimate=pl.CostEstimate(flops=flops, bytes_accessed=nbytes, transcendentals=0),
        **kw,
    )(*args)


def shape(dims, dtype):
    return jax.ShapeDtypeStruct(dims, dtype)


VMEM = pl.BlockSpec(memory_space=pltpu.VMEM)
ANY = pl.BlockSpec(memory_space=pl.ANY)


def load(source, target, sems, i):
    copy = pltpu.make_async_copy(source, target, sems.at[i])
    copy.start()
    return copy


def softmax(logits, axis):
    up = jnp.exp(logits - jnp.max(logits, axis=axis, keepdims=True))
    return up / jnp.sum(up, axis=axis, keepdims=True)


def prep_kernel(
    params_hbm, tokens_hbm, out_grad_hbm, message_ref, dispatch_ref, combine_ref,
    params_ref, tokens_ref, out_grad_ref, sems,
):
    frames = tokens_ref.shape[0]
    rows = message_ref.shape[0]
    copies = [load(params_hbm, params_ref, sems, 2 * frames)]
    copies += [load(tokens_hbm.at[f], tokens_ref.at[f], sems, f) for f in range(frames)]
    copies += [load(out_grad_hbm.at[f], out_grad_ref.at[f], sems, frames + f) for f in range(frames)]
    order = one_hot(
        message_rows((rows, rows), 0, lax.axis_index("yl"), frames, 2)
        == lax.broadcasted_iota(jnp.int32, (rows, rows), 1)
    )
    copies[0].wait()
    slots_in, slot_grad = [], []
    for f in range(frames):
        copies[1 + f].wait()
        tokens = tokens_ref[f]
        logits = dot(tokens, params_ref[...])
        dispatch = softmax(logits, 0)
        combine = softmax(logits, 1)
        dispatch_ref[f] = dispatch
        combine_ref[f] = combine
        slots_in.append(dot(dispatch.astype(bf16), tokens, ((0,), (0,))).astype(bf16))
        copies[1 + frames + f].wait()
        slot_grad.append(dot(combine.astype(bf16), out_grad_ref[f], ((0,), (0,))).astype(bf16))
    message_ref[...] = dot(order, jnp.concatenate(slots_in + slot_grad, axis=0)).astype(bf16)


def sort_order(rows, frames, arrays, axis):
    row = lax.broadcasted_iota(jnp.int32, (rows, rows), axis)
    kinds = 4 * arrays
    kind = row // (rows // kinds)
    rest = row - kind * (rows // kinds)
    return (rest // frames) * (kinds * frames) + kind * frames + (rest & (frames - 1))


def sort_kernel(frames, message_ref, *out_refs):
    rows, depth = message_ref.shape
    order = one_hot(
        sort_order(rows, frames, 2, 0) == lax.broadcasted_iota(jnp.int32, (rows, rows), 1)
    )
    out = dot(order, message_ref[...]).astype(bf16)
    part = rows // len(out_refs)
    for i, out_ref in enumerate(out_refs):
        out_ref[...] = out[i * part : (i + 1) * part].reshape(out_ref.shape)


def unsort_kernel(frames, own_ref, across_ref, back_ref, ahead_ref, message_ref):
    rows, depth = message_ref.shape

    def total(a, b):
        value = a[...].astype(f32) + b[...].astype(f32)
        return value.reshape(rows // 2, depth).astype(bf16)

    value = jnp.concatenate([total(own_ref, across_ref), total(back_ref, ahead_ref)], axis=0)
    order = one_hot(
        sort_order(rows, frames, 1, 1) == lax.broadcasted_iota(jnp.int32, (rows, rows), 0)
    )
    message_ref[...] = dot(order, value).astype(bf16)


def expert_kernel(count, *refs):
    pieces, w_in_ref, w_out_ref = refs[:count], refs[count], refs[count + 1]
    rows_ref, grads_ref, active_ref, pre_ref, partial_ref = refs[-5:]
    rows = jnp.concatenate([piece[0, 0] for piece in pieces], axis=0)
    grads = jnp.concatenate([piece[1, 0] for piece in pieces], axis=0)
    rows_ref[0] = rows
    grads_ref[0] = grads
    hidden = dot(rows, w_in_ref[0])
    act_grad = dot(grads, w_out_ref[0], ((1,), (1,)))
    cdf = 0.5 * (1.0 + lax.erf(hidden * inv_root_two))
    dens = jnp.exp(-0.5 * hidden * hidden) * inv_root_tau
    active_ref[0] = (hidden * cdf).astype(bf16)
    pre = (act_grad * (cdf + hidden * dens)).astype(bf16)
    pre_ref[0] = pre
    partial = dot(pre, w_in_ref[0], ((1,), (1,)))
    partial_ref[...] = partial.astype(partial_ref.dtype).reshape(partial_ref.shape)


def tail_kernel(
    message_ref, tokens_ref, dispatch_ref, part_ref, slots_ref, low_ref, total_ref
):
    rows, depth = message_ref.shape
    frames, experts = slots_ref.shape[:2]
    order = one_hot(
        message_rows((rows, rows), 1, lax.axis_index("yl"), frames, 1)
        == lax.broadcasted_iota(jnp.int32, (rows, rows), 0)
    )
    slots = dot(order, message_ref[...]).astype(bf16)
    total = None
    for f in range(frames):
        mine = slots[f * experts : (f + 1) * experts]
        slots_ref[f] = mine
        tokens = tokens_ref[f]
        dispatch = dispatch_ref[f]
        slope = dot(tokens, mine, ((1,), (1,)))
        slope = slope - jnp.sum(dispatch * slope, axis=0, keepdims=True)
        low = (dispatch * slope + part_ref[f]).astype(bf16)
        low_ref[f] = low
        term = dot(low, tokens, ((0,), (0,)))
        total = term if total is None else total + term
    total_ref[...] = total.T.astype(bf16)


def tokens_kernel(dispatch_ref, low_ref, slots_ref, params_ref, out_ref):
    params = params_ref[...].T
    for f in range(out_ref.shape[0]):
        left = jnp.concatenate([dispatch_ref[f].astype(bf16), low_ref[f]], axis=1)
        right = jnp.concatenate([slots_ref[f], params], axis=0)
        out_ref[f] = dot(left, right).astype(bf16)


def to_y(value, step):
    return lax.ppermute(value, Y, [(i, (i + step) % 4) for i in range(4)])


def to_core(value):
    return lax.ppermute(value, "core", CORE_SWAP)


def exchange(value, axes=ZX):
    return lax.all_to_all(value, axes, split_axis=0, concat_axis=0, tiled=True)


def sum_all(value, beside):
    rows, cols = value.shape
    peers, height = lax.axis_size(PLANE), lax.axis_size("z")
    value = exchange(value.reshape(peers, rows // peers, cols), PLANE)
    value, beside = lax.optimization_barrier((value, beside))
    value = jnp.sum(value.astype(f32), axis=0).astype(bf16)
    value = exchange(jnp.broadcast_to(value[None], (height,) + value.shape), "z")
    value = jnp.sum(value.astype(f32), axis=0).astype(bf16)
    value = exchange(jnp.broadcast_to(value[None], (peers,) + value.shape), PLANE)
    return value.reshape(rows, cols).astype(f32), beside


def shards(tokens, slot_params, w_in, w_out, slot_outputs, out_grad):
    frames, patch, depth = tokens.shape
    experts = slot_params.shape[1]
    hidden_size = w_in.shape[2]
    groups = experts // 4
    rows = frames * experts
    block = rows // 4
    frame_flops = 2 * frames * patch * experts * depth
    sort_flops = 2 * rows * rows * depth

    message, dispatch, combine = call(
        prep_kernel,
        (
            shape((2 * rows, depth), bf16),
            shape((frames, patch, experts), f32),
            shape((frames, patch, experts), f32),
        ),
        slot_params, tokens, out_grad,
        in_specs=[ANY, ANY, ANY], vmem=56, flops=3 * frame_flops + 4 * sort_flops,
        scratch_shapes=[
            pltpu.VMEM((depth, experts), bf16),
            pltpu.VMEM((frames, patch, depth), bf16),
            pltpu.VMEM((frames, patch, depth), bf16),
            pltpu.SemaphoreType.DMA((2 * frames + 1,)),
        ],
    )
    message = exchange(message.reshape(groups, 2 * rows // groups, depth)).reshape(2 * rows, depth)

    combine_grad = jnp.einsum(
        "fpd,fed->fpe", out_grad, slot_outputs, preferred_element_type=f32
    )
    combine_part = combine * (
        combine_grad - jnp.sum(combine * combine_grad, axis=2, keepdims=True)
    )
    message, combine_part = lax.optimization_barrier((message, combine_part))

    own, other = call(
        functools.partial(sort_kernel, frames), (shape((2, 2, block, depth), bf16),) * 2, message,
        flops=4 * sort_flops,
    )
    near = [own, to_y(other, 1), to_y(other, -1), to_y(own, 2)]
    far = [to_core(piece) for piece in near]

    piece = pl.BlockSpec((2, 1, block, depth), lambda e: (0, e, 0, 0))
    w_in_spec = pl.BlockSpec((1, depth, hidden_size), lambda e: (e, 0, 0))
    w_out_spec = pl.BlockSpec((1, hidden_size, depth), lambda e: (e, 0, 0))
    matmul_flops = 2 * 2 * 4 * block * depth * hidden_size

    def expert_half(half, pieces, filled):
        rows_spec = pl.BlockSpec((1, 4 * block, depth), lambda e: (e, half, 0))
        hidden_spec = pl.BlockSpec((1, 4 * block, hidden_size), lambda e: (e, half, 0))
        return call(
            functools.partial(expert_kernel, 4),
            (
                shape((2, 8 * block, depth), bf16),
                shape((2, 8 * block, depth), bf16),
                shape((2, 8 * block, hidden_size), bf16),
                shape((2, 8 * block, hidden_size), bf16),
                shape((4, 2, block, depth), bf16 if half else f32),
            ),
            *pieces, w_in, w_out, *filled,
            grid=(2,),
            in_specs=[piece] * 4 + [w_in_spec, w_out_spec] + [ANY] * len(filled),
            out_specs=(
                rows_spec,
                rows_spec,
                hidden_spec,
                hidden_spec,
                pl.BlockSpec((4, 1, block, depth), lambda e: (0, e, 0, 0)),
            ),
            vmem=24, flops=3 * matmul_flops,
            input_output_aliases={6 + i: i for i in range(len(filled))},
        )

    *filled, near = expert_half(0, near, ())
    near, far[1] = lax.optimization_barrier((near, far[1]))
    slot_rows, grad_rows, active, pre_grad, far = expert_half(1, far, filled)
    far = to_core(far)

    def summed(i):
        return (near[i] + far[i].astype(f32)).astype(bf16)

    back, ahead, across, own = summed(1), summed(2), summed(3), summed(0)
    back, ahead, across = to_y(back, -1), to_y(ahead, 1), to_y(across, 2)
    w_out_grad = jnp.einsum(
        "erh,erd->ehd", active, grad_rows, preferred_element_type=f32
    ).astype(bf16)
    w_in_grad = jnp.einsum(
        "erd,erh->edh", slot_rows, pre_grad, preferred_element_type=f32
    ).astype(bf16)
    own, w_in_grad = lax.optimization_barrier((own, w_in_grad))
    message = call(
        functools.partial(unsort_kernel, frames), shape((rows, depth), bf16),
        own, across, back, ahead, flops=sort_flops,
    )
    message = exchange(message.reshape(groups, rows // groups, depth)).reshape(rows, depth)
    message, w_out_grad = lax.optimization_barrier((message, w_out_grad))

    slots_in_grad, logits_low, total = call(
        tail_kernel,
        (
            shape((frames, experts, depth), bf16),
            shape((frames, patch, experts), bf16),
            shape((depth, experts), bf16),
        ),
        message, tokens, dispatch, combine_part, flops=2 * frame_flops + sort_flops,
    )
    tokens_grad = call(
        tokens_kernel, shape((frames, patch, depth), bf16),
        dispatch, logits_low, slots_in_grad, slot_params, flops=2 * frame_flops,
    )
    params_grad, tokens_grad = sum_all(total, tokens_grad)
    return (tokens_grad, params_grad, w_in_grad, w_out_grad)


def split_mesh(mesh):
    experts = mesh.devices.shape[1]
    x = 4 if experts >= 64 else 2
    return Mesh(
        mesh.devices.reshape(2, 2, experts // (2 * x), x, 2), ("yh", "core", "z", "x", "yl")
    )


def solution(mesh):
    dp, expert = ("yh", "core"), ("z", "x", "yl")
    whole = dp + expert
    in_specs = (
        P(whole, None, None),
        P(),
        P(expert, None, dp),
        P(expert, dp, None),
        P(whole, None, None),
        P(whole, None, None),
    )
    out_specs = (
        P(whole, None, None),
        P(),
        P(expert, None, dp),
        P(expert, dp, None),
    )
    return jax.shard_map(
        shards, mesh=split_mesh(mesh), in_specs=in_specs, out_specs=out_specs, check_vma=False
    )
```

```python
import functools

import jax
import jax.numpy as jnp
from jax import lax
from jax.experimental import pallas as pl
from jax.experimental.pallas import tpu as pltpu
from jax.sharding import Mesh, PartitionSpec as P

inv_root_two = 0.7071067811865476
inv_root_tau = 0.3989422804014327

bf16 = jnp.bfloat16
f32 = jnp.float32
Y = ("yh", "yl")
ZX = ("z", "x")
PLANE = ("yh", "core", "x", "yl")
CORE_SWAP = [(0, 1), (1, 0)]
MIB = 1 << 20


def dot(a, b, dims=((1,), (0,))):
    return lax.dot_general(a, b, (dims, ((), ())), preferred_element_type=f32)


def one_hot(test):
    return jnp.where(test, 1.0, 0.0).astype(bf16)


def message_rows(shape, axis, yl, frames, arrays):
    row = lax.broadcasted_iota(jnp.int32, shape, axis)
    experts = shape[axis] // (frames * arrays)
    frame = row & (frames - 1)
    rest = row // frames
    pair = rest & 1
    array = (rest // 2) & (arrays - 1)
    rest = rest // (2 * arrays)
    expert = (rest // 2) * 4 + ((rest & 1) ^ yl) * 2 + pair
    return (array * frames + frame) * experts + expert


def call(kernel, out_shape, *args, grid=(), in_specs=None, out_specs=None, vmem=16, flops=0, **kw):
    nbytes = sum(a.size * a.dtype.itemsize for a in args)
    nbytes += sum(o.size * o.dtype.itemsize for o in jax.tree.leaves(out_shape))
    if in_specs is None:
        in_specs = [pl.BlockSpec(memory_space=pltpu.VMEM) for _ in args]
    if out_specs is None:
        out_specs = jax.tree.map(lambda _: pl.BlockSpec(memory_space=pltpu.VMEM), out_shape)
    return pl.pallas_call(
        kernel,
        out_shape=out_shape,
        grid=grid,
        in_specs=in_specs,
        out_specs=out_specs,
        compiler_params=pltpu.CompilerParams(vmem_limit_bytes=vmem * MIB),
        cost_estimate=pl.CostEstimate(flops=flops, bytes_accessed=nbytes, transcendentals=0),
        **kw,
    )(*args)


def shape(dims, dtype):
    return jax.ShapeDtypeStruct(dims, dtype)


VMEM = pl.BlockSpec(memory_space=pltpu.VMEM)
ANY = pl.BlockSpec(memory_space=pl.ANY)


def load(source, target, sems, i):
    copy = pltpu.make_async_copy(source, target, sems.at[i])
    copy.start()
    return copy


def softmax(logits, axis):
    up = jnp.exp(logits - jnp.max(logits, axis=axis, keepdims=True))
    return up / jnp.sum(up, axis=axis, keepdims=True)


def prep_kernel(
    params_hbm, tokens_hbm, out_grad_hbm, message_ref, dispatch_ref, combine_ref,
    params_ref, tokens_ref, out_grad_ref, sems,
):
    frames = tokens_ref.shape[0]
    rows = message_ref.shape[0]
    copies = [load(params_hbm, params_ref, sems, 2 * frames)]
    copies += [load(tokens_hbm.at[f], tokens_ref.at[f], sems, f) for f in range(frames)]
    copies += [load(out_grad_hbm.at[f], out_grad_ref.at[f], sems, frames + f) for f in range(frames)]
    half = rows // 2
    order = one_hot(
        message_rows((half, half), 0, lax.axis_index("yl"), frames, 2)
        == lax.broadcasted_iota(jnp.int32, (half, half), 1)
    )
    copies[0].wait()
    slots_in, slot_grad = [], []
    for f in range(frames):
        copies[1 + f].wait()
        tokens = tokens_ref[f]
        logits = dot(tokens, params_ref[...])
        dispatch = softmax(logits, 0)
        combine = softmax(logits, 1)
        dispatch_ref[f] = dispatch
        combine_ref[f] = combine
        slots_in.append(dot(dispatch.astype(bf16), tokens, ((0,), (0,))).astype(bf16))
        copies[1 + frames + f].wait()
        slot_grad.append(dot(combine.astype(bf16), out_grad_ref[f], ((0,), (0,))).astype(bf16))
    part = half // (2 * frames)
    for i in range(2):
        value = jnp.concatenate([slots[i * part : (i + 1) * part] for slots in slots_in + slot_grad], axis=0)
        message_ref[i * half : (i + 1) * half, :] = dot(order, value).astype(bf16)


def sort_order(rows, frames, arrays, axis):
    row = lax.broadcasted_iota(jnp.int32, (rows, rows), axis)
    kinds = 4 * arrays
    kind = row // (rows // kinds)
    rest = row - kind * (rows // kinds)
    return (rest // frames) * (kinds * frames) + kind * frames + (rest & (frames - 1))


def sort_kernel(frames, message_ref, _, own_ref, other_ref):
    half = message_ref.shape[0] // 2
    order = one_hot(
        sort_order(half, frames, 2, 0) == lax.broadcasted_iota(jnp.int32, (half, half), 1)
    )
    part = half // 8
    for i in range(2):
        out = dot(order, message_ref[i * half : (i + 1) * half, :]).astype(bf16)
        for kind in range(8):
            rel, array, e2 = kind // 4, kind // 2 % 2, kind % 2
            target = (own_ref, other_ref)[rel]
            target[array, e2, i * part : (i + 1) * part, :] = out[kind * part : (kind + 1) * part]


def unsort_kernel(frames, own_ref, across_ref, back_ref, ahead_ref, message_ref):
    rows, depth = message_ref.shape

    def total(a, b):
        value = a[...].astype(f32) + b[...].astype(f32)
        return value.reshape(rows // 2, depth).astype(bf16)

    value = jnp.concatenate([total(own_ref, across_ref), total(back_ref, ahead_ref)], axis=0)
    order = one_hot(
        sort_order(rows, frames, 1, 1) == lax.broadcasted_iota(jnp.int32, (rows, rows), 0)
    )
    message_ref[...] = dot(order, value).astype(bf16)


def expert_kernel(count, *refs):
    pieces, w_in_ref, w_out_ref = refs[:count], refs[count], refs[count + 1]
    rows_ref, grads_ref, active_ref, pre_ref, partial_ref = refs[-5:]
    rows = jnp.concatenate([piece[0, 0] for piece in pieces], axis=0)
    grads = jnp.concatenate([piece[1, 0] for piece in pieces], axis=0)
    rows_ref[0] = rows
    grads_ref[0] = grads
    hidden = dot(rows, w_in_ref[0])
    act_grad = dot(grads, w_out_ref[0], ((1,), (1,)))
    cdf = 0.5 * (1.0 + lax.erf(hidden * inv_root_two))
    dens = jnp.exp(-0.5 * hidden * hidden) * inv_root_tau
    active_ref[0] = (hidden * cdf).astype(bf16)
    pre = (act_grad * (cdf + hidden * dens)).astype(bf16)
    pre_ref[0] = pre
    partial = dot(pre, w_in_ref[0], ((1,), (1,)))
    partial_ref[...] = partial.astype(partial_ref.dtype).reshape(partial_ref.shape)


def tail_kernel(
    message_ref, tokens_ref, dispatch_ref, part_ref, slots_ref, low_ref, total_ref
):
    rows, depth = message_ref.shape
    frames, experts = slots_ref.shape[:2]
    order = one_hot(
        message_rows((rows, rows), 1, lax.axis_index("yl"), frames, 1)
        == lax.broadcasted_iota(jnp.int32, (rows, rows), 0)
    )
    slots = dot(order, message_ref[...]).astype(bf16)
    total = None
    for f in range(frames):
        mine = slots[f * experts : (f + 1) * experts]
        slots_ref[f] = mine
        tokens = tokens_ref[f]
        dispatch = dispatch_ref[f]
        slope = dot(tokens, mine, ((1,), (1,)))
        slope = slope - jnp.sum(dispatch * slope, axis=0, keepdims=True)
        low = (dispatch * slope + part_ref[f]).astype(bf16)
        low_ref[f] = low
        term = dot(low, tokens, ((0,), (0,)))
        total = term if total is None else total + term
    total_ref[...] = total.T.astype(bf16)


def tokens_kernel(dispatch_ref, low_ref, slots_ref, params_ref, out_ref):
    params = params_ref[...].T
    for f in range(out_ref.shape[0]):
        left = jnp.concatenate([dispatch_ref[f].astype(bf16), low_ref[f]], axis=1)
        right = jnp.concatenate([slots_ref[f], params], axis=0)
        out_ref[f] = dot(left, right).astype(bf16)


def to_y(value, step):
    return lax.ppermute(value, Y, [(i, (i + step) % 4) for i in range(4)])


def to_core(value):
    return lax.ppermute(value, "core", CORE_SWAP)


def exchange(value, axes=ZX):
    return lax.all_to_all(value, axes, split_axis=0, concat_axis=0, tiled=True)


def sum_all(value, beside):
    rows, cols = value.shape
    peers, height = lax.axis_size(PLANE), lax.axis_size("z")
    value = exchange(value.reshape(peers, rows // peers, cols), PLANE)
    value, beside = lax.optimization_barrier((value, beside))
    value = jnp.sum(value.astype(f32), axis=0).astype(bf16)
    value = exchange(jnp.broadcast_to(value[None], (height,) + value.shape), "z")
    value = jnp.sum(value.astype(f32), axis=0).astype(bf16)
    value = exchange(jnp.broadcast_to(value[None], (peers,) + value.shape), PLANE)
    return value.reshape(rows, cols).astype(f32), beside


def shards(tokens, slot_params, w_in, w_out, slot_outputs, out_grad):
    frames, patch, depth = tokens.shape
    experts = slot_params.shape[1]
    hidden_size = w_in.shape[2]
    groups = experts // 4
    rows = frames * experts
    block = rows // 4
    frame_flops = 2 * frames * patch * experts * depth
    sort_flops = 2 * rows * rows * depth

    message, dispatch, combine = call(
        prep_kernel,
        (
            shape((2 * rows, depth), bf16),
            shape((frames, patch, experts), f32),
            shape((frames, patch, experts), f32),
        ),
        slot_params, tokens, out_grad,
        in_specs=[ANY, ANY, ANY], vmem=56, flops=3 * frame_flops + 4 * sort_flops,
        scratch_shapes=[
            pltpu.VMEM((depth, experts), bf16),
            pltpu.VMEM((frames, patch, depth), bf16),
            pltpu.VMEM((frames, patch, depth), bf16),
            pltpu.SemaphoreType.DMA((2 * frames + 1,)),
        ],
    )
    message = exchange(message.reshape(groups, 2 * rows // groups, depth)).reshape(2 * rows, depth)

    combine_grad = jnp.einsum(
        "fpd,fed->fpe", out_grad, slot_outputs, preferred_element_type=f32
    )
    combine_part = combine * (
        combine_grad - jnp.sum(combine * combine_grad, axis=2, keepdims=True)
    )
    message, combine_part = lax.optimization_barrier((message, combine_part))

    own, other = call(
        functools.partial(sort_kernel, frames), (shape((2, 2, block, depth), bf16),) * 2, message, w_out,
        flops=4 * sort_flops,
    )
    near = [own, to_y(other, 1), to_y(other, -1), to_y(own, 2)]
    far = [to_core(piece) for piece in near]

    piece = pl.BlockSpec((2, 1, block, depth), lambda e: (0, e, 0, 0))
    w_in_spec = pl.BlockSpec((1, depth, hidden_size), lambda e: (e, 0, 0))
    w_out_spec = pl.BlockSpec((1, hidden_size, depth), lambda e: (e, 0, 0))
    matmul_flops = 2 * 2 * 4 * block * depth * hidden_size

    def expert_half(half, pieces, filled):
        rows_spec = pl.BlockSpec((1, 4 * block, depth), lambda e: (e, half, 0))
        hidden_spec = pl.BlockSpec((1, 4 * block, hidden_size), lambda e: (e, half, 0))
        return call(
            functools.partial(expert_kernel, 4),
            (
                shape((2, 8 * block, depth), bf16),
                shape((2, 8 * block, depth), bf16),
                shape((2, 8 * block, hidden_size), bf16),
                shape((2, 8 * block, hidden_size), bf16),
                shape((4, 2, block, depth), bf16 if half else f32),
            ),
            *pieces, w_in, w_out, *filled,
            grid=(2,),
            in_specs=[piece] * 4 + [w_in_spec, w_out_spec] + [ANY] * len(filled),
            out_specs=(
                rows_spec,
                rows_spec,
                hidden_spec,
                hidden_spec,
                pl.BlockSpec((4, 1, block, depth), lambda e: (0, e, 0, 0)),
            ),
            vmem=24, flops=3 * matmul_flops,
            input_output_aliases={6 + i: i for i in range(len(filled))},
        )

    *filled, near = expert_half(0, near, ())
    near, far[1] = lax.optimization_barrier((near, far[1]))
    slot_rows, grad_rows, active, pre_grad, far = expert_half(1, far, filled)
    far = to_core(far)

    def summed(i):
        return (near[i] + far[i].astype(f32)).astype(bf16)

    back, ahead, across, own = summed(1), summed(2), summed(3), summed(0)
    own, slot_rows = lax.optimization_barrier((own, slot_rows))
    back, ahead, across = to_y(back, -1), to_y(ahead, 1), to_y(across, 2)
    w_out_grad = jnp.einsum(
        "erh,erd->ehd", active, grad_rows, preferred_element_type=f32
    ).astype(bf16)
    w_in_grad = jnp.einsum(
        "erd,erh->edh", slot_rows, pre_grad, preferred_element_type=f32
    ).astype(bf16)
    own, w_in_grad, w_out_grad = lax.optimization_barrier((own, w_in_grad, w_out_grad))
    message = call(
        functools.partial(unsort_kernel, frames), shape((rows, depth), bf16),
        own, across, back, ahead, flops=sort_flops,
    )
    message = exchange(message.reshape(groups, rows // groups, depth)).reshape(rows, depth)

    slots_in_grad, logits_low, total = call(
        tail_kernel,
        (
            shape((frames, experts, depth), bf16),
            shape((frames, patch, experts), bf16),
            shape((depth, experts), bf16),
        ),
        message, tokens, dispatch, combine_part, flops=2 * frame_flops + sort_flops,
    )
    tokens_grad = call(
        tokens_kernel, shape((frames, patch, depth), bf16),
        dispatch, logits_low, slots_in_grad, slot_params, flops=2 * frame_flops,
    )
    params_grad, tokens_grad = sum_all(total, tokens_grad)
    return (tokens_grad, params_grad, w_in_grad, w_out_grad)


def split_mesh(mesh):
    experts = mesh.devices.shape[1]
    x = 4 if experts >= 64 else 2
    return Mesh(
        mesh.devices.reshape(2, 2, experts // (2 * x), x, 2), ("yh", "core", "z", "x", "yl")
    )


def solution(mesh):
    dp, expert = ("yh", "core"), ("z", "x", "yl")
    whole = dp + expert
    in_specs = (
        P(whole, None, None),
        P(),
        P(expert, None, dp),
        P(expert, dp, None),
        P(whole, None, None),
        P(whole, None, None),
    )
    out_specs = (
        P(whole, None, None),
        P(),
        P(expert, None, dp),
        P(expert, dp, None),
    )
    return jax.shard_map(
        shards, mesh=split_mesh(mesh), in_specs=in_specs, out_specs=out_specs, check_vma=False
    )
```

```python
import functools

import jax
import jax.numpy as jnp
from jax import lax
from jax.experimental import pallas as pl
from jax.experimental.pallas import tpu as pltpu
from jax.sharding import Mesh, PartitionSpec as P

inv_root_two = 0.7071067811865476
inv_root_tau = 0.3989422804014327

bf16 = jnp.bfloat16
f32 = jnp.float32
Y = ("yh", "yl")
ZX = ("z", "x")
PLANE = ("yh", "core", "x", "yl")
CORE_SWAP = [(0, 1), (1, 0)]
MIB = 1 << 20


def dot(a, b, dims=((1,), (0,))):
    return lax.dot_general(a, b, (dims, ((), ())), preferred_element_type=f32)


def one_hot(test):
    return jnp.where(test, 1.0, 0.0).astype(bf16)


def message_rows(shape, axis, yl, frames, arrays):
    row = lax.broadcasted_iota(jnp.int32, shape, axis)
    experts = shape[axis] // (frames * arrays)
    frame = row & (frames - 1)
    rest = row // frames
    pair = rest & 1
    array = (rest // 2) & (arrays - 1)
    rest = rest // (2 * arrays)
    expert = (rest // 2) * 4 + ((rest & 1) ^ yl) * 2 + pair
    return (array * frames + frame) * experts + expert


def call(kernel, out_shape, *args, grid=(), in_specs=None, out_specs=None, vmem=16, flops=0, **kw):
    nbytes = sum(a.size * a.dtype.itemsize for a in args)
    nbytes += sum(o.size * o.dtype.itemsize for o in jax.tree.leaves(out_shape))
    if in_specs is None:
        in_specs = [pl.BlockSpec(memory_space=pltpu.VMEM) for _ in args]
    if out_specs is None:
        out_specs = jax.tree.map(lambda _: pl.BlockSpec(memory_space=pltpu.VMEM), out_shape)
    return pl.pallas_call(
        kernel,
        out_shape=out_shape,
        grid=grid,
        in_specs=in_specs,
        out_specs=out_specs,
        compiler_params=pltpu.CompilerParams(vmem_limit_bytes=vmem * MIB),
        cost_estimate=pl.CostEstimate(flops=flops, bytes_accessed=nbytes, transcendentals=0),
        **kw,
    )(*args)


def shape(dims, dtype):
    return jax.ShapeDtypeStruct(dims, dtype)


VMEM = pl.BlockSpec(memory_space=pltpu.VMEM)
ANY = pl.BlockSpec(memory_space=pl.ANY)


def load(source, target, sems, i):
    copy = pltpu.make_async_copy(source, target, sems.at[i])
    copy.start()
    return copy


def softmax(logits, axis):
    up = jnp.exp(logits - jnp.max(logits, axis=axis, keepdims=True))
    return up / jnp.sum(up, axis=axis, keepdims=True)


def prep_kernel(
    params_hbm, tokens_hbm, out_grad_hbm, message_ref, dispatch_ref, combine_ref,
    params_ref, tokens_ref, out_grad_ref, sems,
):
    frames = tokens_ref.shape[0]
    rows = message_ref.shape[0]
    copies = [load(params_hbm, params_ref, sems, 2 * frames)]
    copies += [load(tokens_hbm.at[f], tokens_ref.at[f], sems, f) for f in range(frames)]
    copies += [load(out_grad_hbm.at[f], out_grad_ref.at[f], sems, frames + f) for f in range(frames)]
    half = rows // 2
    order = one_hot(
        message_rows((half, half), 0, lax.axis_index("yl"), frames, 2)
        == lax.broadcasted_iota(jnp.int32, (half, half), 1)
    )
    copies[0].wait()
    slots_in, slot_grad = [], []
    for f in range(frames):
        copies[1 + f].wait()
        tokens = tokens_ref[f]
        logits = dot(tokens, params_ref[...])
        dispatch = softmax(logits, 0)
        combine = softmax(logits, 1)
        dispatch_ref[f] = dispatch
        combine_ref[f] = combine
        slots_in.append(dot(dispatch.astype(bf16), tokens, ((0,), (0,))).astype(bf16))
        copies[1 + frames + f].wait()
        slot_grad.append(dot(combine.astype(bf16), out_grad_ref[f], ((0,), (0,))).astype(bf16))
    part = half // (2 * frames)
    for i in range(2):
        value = jnp.concatenate([slots[i * part : (i + 1) * part] for slots in slots_in + slot_grad], axis=0)
        message_ref[i * half : (i + 1) * half, :] = dot(order, value).astype(bf16)


def sort_order(rows, frames, arrays, axis):
    row = lax.broadcasted_iota(jnp.int32, (rows, rows), axis)
    kinds = 4 * arrays
    kind = row // (rows // kinds)
    rest = row - kind * (rows // kinds)
    return (rest // frames) * (kinds * frames) + kind * frames + (rest & (frames - 1))


def sort_kernel(frames, message_ref, _, own_ref, other_ref):
    half = message_ref.shape[0] // 2
    order = one_hot(
        sort_order(half, frames, 2, 0) == lax.broadcasted_iota(jnp.int32, (half, half), 1)
    )
    part = half // 8
    for i in range(2):
        out = dot(order, message_ref[i * half : (i + 1) * half, :]).astype(bf16)
        for kind in range(8):
            rel, array, e2 = kind // 4, kind // 2 % 2, kind % 2
            target = (own_ref, other_ref)[rel]
            target[array, e2, i * part : (i + 1) * part, :] = out[kind * part : (kind + 1) * part]


def unsort_kernel(frames, own_ref, across_ref, back_ref, ahead_ref, message_ref):
    rows, depth = message_ref.shape

    def total(a, b):
        value = a[...].astype(f32) + b[...].astype(f32)
        return value.reshape(rows // 2, depth).astype(bf16)

    value = jnp.concatenate([total(own_ref, across_ref), total(back_ref, ahead_ref)], axis=0)
    order = one_hot(
        sort_order(rows, frames, 1, 1) == lax.broadcasted_iota(jnp.int32, (rows, rows), 0)
    )
    message_ref[...] = dot(order, value).astype(bf16)


def expert_kernel(count, *refs):
    pieces, w_in_ref, w_out_back_ref = refs[:count], refs[count], refs[count + 1]
    rows_ref, grads_ref, active_ref, pre_ref, partial_ref = refs[-5:]
    rows = jnp.concatenate([piece[0, 0] for piece in pieces], axis=0)
    grads = jnp.concatenate([piece[1, 0] for piece in pieces], axis=0)
    rows_ref[0] = rows
    grads_ref[0] = grads
    hidden = dot(rows, w_in_ref[0])
    act_grad = dot(grads, w_out_back_ref[0])
    cdf = 0.5 * (1.0 + lax.erf(hidden * inv_root_two))
    dens = jnp.exp(-0.5 * hidden * hidden) * inv_root_tau
    active_ref[0] = (hidden * cdf).astype(bf16)
    pre = (act_grad * (cdf + hidden * dens)).astype(bf16)
    pre_ref[0] = pre
    partial = dot(pre, w_in_ref[0], ((1,), (1,)))
    partial_ref[...] = partial.astype(partial_ref.dtype).reshape(partial_ref.shape)


def tail_kernel(
    message_ref, tokens_ref, dispatch_ref, part_ref, slots_ref, low_ref, total_ref
):
    rows, depth = message_ref.shape
    frames, experts = slots_ref.shape[:2]
    order = one_hot(
        message_rows((rows, rows), 1, lax.axis_index("yl"), frames, 1)
        == lax.broadcasted_iota(jnp.int32, (rows, rows), 0)
    )
    slots = dot(order, message_ref[...]).astype(bf16)
    total = None
    for f in range(frames):
        mine = slots[f * experts : (f + 1) * experts]
        slots_ref[f] = mine
        tokens = tokens_ref[f]
        dispatch = dispatch_ref[f]
        slope = dot(tokens, mine, ((1,), (1,)))
        slope = slope - jnp.sum(dispatch * slope, axis=0, keepdims=True)
        low = (dispatch * slope + part_ref[f]).astype(bf16)
        low_ref[f] = low
        term = dot(low, tokens, ((0,), (0,)))
        total = term if total is None else total + term
    total_ref[...] = total.T.astype(bf16)


def tokens_kernel(dispatch_ref, low_ref, slots_ref, params_ref, out_ref):
    params = params_ref[...].T
    for f in range(out_ref.shape[0]):
        left = jnp.concatenate([dispatch_ref[f].astype(bf16), low_ref[f]], axis=1)
        right = jnp.concatenate([slots_ref[f], params], axis=0)
        out_ref[f] = dot(left, right).astype(bf16)


def to_y(value, step):
    return lax.ppermute(value, Y, [(i, (i + step) % 4) for i in range(4)])


def to_core(value):
    return lax.ppermute(value, "core", CORE_SWAP)


def exchange(value, axes=ZX):
    return lax.all_to_all(value, axes, split_axis=0, concat_axis=0, tiled=True)


def sum_all(value, beside):
    rows, cols = value.shape
    peers, height = lax.axis_size(PLANE), lax.axis_size("z")
    value = exchange(value.reshape(peers, rows // peers, cols), PLANE)
    value, beside = lax.optimization_barrier((value, beside))
    value = jnp.sum(value.astype(f32), axis=0).astype(bf16)
    value = exchange(jnp.broadcast_to(value[None], (height,) + value.shape), "z")
    value = jnp.sum(value.astype(f32), axis=0).astype(bf16)
    value = exchange(jnp.broadcast_to(value[None], (peers,) + value.shape), PLANE)
    return value.reshape(rows, cols).astype(f32), beside


def shards(tokens, slot_params, w_in, w_out, slot_outputs, out_grad):
    frames, patch, depth = tokens.shape
    experts = slot_params.shape[1]
    hidden_size = w_in.shape[2]
    groups = experts // 4
    rows = frames * experts
    block = rows // 4
    frame_flops = 2 * frames * patch * experts * depth
    sort_flops = 2 * rows * rows * depth

    message, dispatch, combine = call(
        prep_kernel,
        (
            shape((2 * rows, depth), bf16),
            shape((frames, patch, experts), f32),
            shape((frames, patch, experts), f32),
        ),
        slot_params, tokens, out_grad,
        in_specs=[ANY, ANY, ANY], vmem=56, flops=3 * frame_flops + 4 * sort_flops,
        scratch_shapes=[
            pltpu.VMEM((depth, experts), bf16),
            pltpu.VMEM((frames, patch, depth), bf16),
            pltpu.VMEM((frames, patch, depth), bf16),
            pltpu.SemaphoreType.DMA((2 * frames + 1,)),
        ],
    )
    message = exchange(message.reshape(groups, 2 * rows // groups, depth)).reshape(2 * rows, depth)

    combine_grad = jnp.einsum(
        "fpd,fed->fpe", out_grad, slot_outputs, preferred_element_type=f32
    )
    combine_part = combine * (
        combine_grad - jnp.sum(combine * combine_grad, axis=2, keepdims=True)
    )
    w_out_back = jnp.swapaxes(w_out, 1, 2)
    message, combine_part, w_out_back = lax.optimization_barrier((message, combine_part, w_out_back))

    own, other = call(
        functools.partial(sort_kernel, frames), (shape((2, 2, block, depth), bf16),) * 2, message, w_out_back,
        flops=4 * sort_flops,
    )
    near = [own, to_y(other, 1), to_y(other, -1), to_y(own, 2)]
    far = [to_core(piece) for piece in near]

    piece = pl.BlockSpec((2, 1, block, depth), lambda e: (0, e, 0, 0))
    w_in_spec = pl.BlockSpec((1, depth, hidden_size), lambda e: (e, 0, 0))
    matmul_flops = 2 * 2 * 4 * block * depth * hidden_size

    def expert_half(half, pieces, filled):
        rows_spec = pl.BlockSpec((1, 4 * block, depth), lambda e: (e, half, 0))
        hidden_spec = pl.BlockSpec((1, 4 * block, hidden_size), lambda e: (e, half, 0))
        return call(
            functools.partial(expert_kernel, 4),
            (
                shape((2, 8 * block, depth), bf16),
                shape((2, 8 * block, depth), bf16),
                shape((2, 8 * block, hidden_size), bf16),
                shape((2, 8 * block, hidden_size), bf16),
                shape((4, 2, block, depth), bf16 if half else f32),
            ),
            *pieces, w_in, w_out_back, *filled,
            grid=(2,),
            in_specs=[piece] * 4 + [w_in_spec, w_in_spec] + [ANY] * len(filled),
            out_specs=(
                rows_spec,
                rows_spec,
                hidden_spec,
                hidden_spec,
                pl.BlockSpec((4, 1, block, depth), lambda e: (0, e, 0, 0)),
            ),
            vmem=24, flops=3 * matmul_flops,
            input_output_aliases={6 + i: i for i in range(len(filled))},
        )

    *filled, near = expert_half(0, near, ())
    near, far[1] = lax.optimization_barrier((near, far[1]))
    slot_rows, grad_rows, active, pre_grad, far = expert_half(1, far, filled)
    far = to_core(far)

    def summed(i):
        return (near[i] + far[i].astype(f32)).astype(bf16)

    back, ahead, across, own = summed(1), summed(2), summed(3), summed(0)
    own, slot_rows, active = lax.optimization_barrier((own, slot_rows, active))
    back, ahead, across = to_y(back, -1), to_y(ahead, 1), to_y(across, 2)
    w_out_grad = jnp.einsum(
        "erh,erd->ehd", active, grad_rows, preferred_element_type=f32
    ).astype(bf16)
    w_in_grad = jnp.einsum(
        "erd,erh->edh", slot_rows, pre_grad, preferred_element_type=f32
    ).astype(bf16)
    own, w_in_grad, w_out_grad = lax.optimization_barrier((own, w_in_grad, w_out_grad))
    message = call(
        functools.partial(unsort_kernel, frames), shape((rows, depth), bf16),
        own, across, back, ahead, flops=sort_flops,
    )
    message = exchange(message.reshape(groups, rows // groups, depth)).reshape(rows, depth)

    slots_in_grad, logits_low, total = call(
        tail_kernel,
        (
            shape((frames, experts, depth), bf16),
            shape((frames, patch, experts), bf16),
            shape((depth, experts), bf16),
        ),
        message, tokens, dispatch, combine_part, flops=2 * frame_flops + sort_flops,
    )
    tokens_grad = call(
        tokens_kernel, shape((frames, patch, depth), bf16),
        dispatch, logits_low, slots_in_grad, slot_params, flops=2 * frame_flops,
    )
    params_grad, tokens_grad = sum_all(total, tokens_grad)
    return (tokens_grad, params_grad, w_in_grad, w_out_grad)


def split_mesh(mesh):
    experts = mesh.devices.shape[1]
    x = 4 if experts >= 64 else 2
    return Mesh(
        mesh.devices.reshape(2, 2, experts // (2 * x), x, 2), ("yh", "core", "z", "x", "yl")
    )


def solution(mesh):
    dp, expert = ("yh", "core"), ("z", "x", "yl")
    whole = dp + expert
    in_specs = (
        P(whole, None, None),
        P(),
        P(expert, None, dp),
        P(expert, dp, None),
        P(whole, None, None),
        P(whole, None, None),
    )
    out_specs = (
        P(whole, None, None),
        P(),
        P(expert, None, dp),
        P(expert, dp, None),
    )
    return jax.shard_map(
        shards, mesh=split_mesh(mesh), in_specs=in_specs, out_specs=out_specs, check_vma=False
    )
```
